1024 devices in a mesh: tok: 4 (over z_hi), fin: 16 (over y, core), fout: 16 (over z_lo, x).
Axes of the slice: x: 8, y: 8, z: 8 (z_hi: 4, z_lo: 2; z = z_hi * 2 + z_lo), core: 2. Of those that a mesh axis runs over, the one named last changes fastest.
Arguments:
- acts: float32 [2048, 12288], P('tok', 'fin'), may hold values from -6 to 6
- weight: float32 [12288, 12288], P(('fin', 'tok'), 'fout'), may hold values from -0.0546875 to 0.0546875
- grad_out: float32 [2048, 12288], P(('tok', 'fin'), 'fout'), may hold values from -6 to 6
Outputs:
- outputs: float32 [2048, 12288], P(('tok', 'fin'), 'fout')
- grad_acts: float32 [2048, 12288], P(('tok', 'fout'), 'fin')
- grad_weight: float32 [12288, 12288], P(('fin', 'tok'), 'fout')
The draws below stay inside these ranges and needn't reach their ends.
All inputs are finite; a program needn't handle non-finite values.
Results may differ from the reference program's by a relative error of at most 0.000075.
Values sent between devices are 32-bit elements; how exact they have to be, the bound alone decides.
A program may use at most 32 MiB of HBM per device.

```python
import jax
import jax.numpy as jnp
from jax import lax

D = 12288
TOKENS = 2048


def block_scale(stream_key, extent, split, least, top_value):
    factor_of = 1.0
    for position, shards_of in split:
        steps = jax.random.uniform(jax.random.fold_in(jax.random.fold_in(stream_key, 6), position), (shards_of,), jnp.float32, least / len(split), top_value / len(split))
        factor_of = factor_of * jnp.repeat(jnp.exp(steps), extent[position] // shards_of).reshape((-1,) + (1,) * (len(extent) - 1 - position))
    return factor_of


def bell_draw(rng, shape, deviation, limit, pieces=(), dtype=jnp.bfloat16):
    loudness = block_scale(rng, shape, pieces, -0.22, 0.18) if pieces else 1.0
    result = jax.random.normal(rng, shape, jnp.float32) * deviation * loudness
    return jnp.minimum(jnp.maximum(result, -limit), limit).astype(dtype)


def setup_inputs(seed: int = 0) -> dict:
    streams_of = jax.random.split(jax.random.key(seed), 4)
    return {
        "acts": bell_draw(streams_of[0], (TOKENS, D), 1.0, 6.0, ((0, 4), (1, 16)), jnp.float32),
        "weight": bell_draw(streams_of[1], (D, D), D ** -0.5, 0.0546875, ((0, 64), (1, 16)), jnp.float32),
        "grad_out": bell_draw(streams_of[2], (TOKENS, D), 1.0, 6.0, ((0, 64), (1, 16)), jnp.float32),
    }


def reference(acts, weight, grad_out):
    high = lax.Precision.HIGHEST
    outputs = jnp.dot(acts, weight, precision=high, preferred_element_type=jnp.float32)
    grad_acts = jnp.dot(grad_out, weight.T, precision=high, preferred_element_type=jnp.float32)
    grad_weight = jnp.dot(acts.T, grad_out, precision=high, preferred_element_type=jnp.float32)
    return outputs, grad_acts, grad_weight
```

```python
import functools

import jax
import jax.numpy as jnp
from jax import lax
from jax.experimental import pallas as pl
from jax.experimental.pallas import tpu as pltpu
from jax.sharding import PartitionSpec as P

MESH = pl.DeviceIdType.MESH
F32 = jnp.float32


def halves(value):
    high = value.astype(jnp.bfloat16)
    return high, (value - high.astype(F32)).astype(jnp.bfloat16)


def dot3(left, right, left_dim, right_dim):
    dims = (((left_dim,), (right_dim,)), ((), ()))
    dot = functools.partial(lax.dot_general, dimension_numbers=dims, preferred_element_type=F32)
    return dot(left[0], right[0]) + (dot(left[0], right[1]) + dot(left[1], right[0]))


def kernel(sizes, acts, weight, grad, out, grad_acts, grad_weight,
           acts_t, acts_hi, acts_lo, cols, grads, tile, part, part_in, y_up, y_dn, gpart, x_up, x_dn, swap, swap_in,
           send_sem, recv_sem):
    n_tok, n_fin, n_fout = sizes
    n_y, n_x = n_fin // 2, n_fout // 2
    t, i, o = lax.axis_index("tok"), lax.axis_index("fin"), lax.axis_index("fout")
    y, c = i // 2, lax.rem(i, 2)
    zl, x = o // n_x, lax.rem(o, n_x)
    z_up, z_dn, z_op = [(lax.rem(t + d, n_tok), i, o) for d in (1, n_tok - 1, 2)]
    yu, yd = [(t, lax.rem(i + d, n_fin), o) for d in (2, n_fin - 2)]
    core = (t, i + 1 - 2 * c, o)
    xu, xd = [(t, i, zl * n_x + lax.rem(x + d, n_x)) for d in (1, n_x - 1)]
    zlo = (t, i, lax.rem(o + n_x, n_fout))
    rows = grad.shape[0]
    w_rows = weight.shape[0]
    piece = w_rows // n_x
    quarter = w_rows // 4

    barrier = pltpu.get_barrier_semaphore()
    peers = (z_up, z_dn, z_op, yu, yd, core, xu, xd, zlo)
    for peer in peers:
        pl.semaphore_signal(barrier, inc=1, device_id=peer, device_id_type=MESH)
    pl.semaphore_wait(barrier, len(peers))

    started = []

    def copy(src, dst, peer):
        k = len(started)
        cp = pltpu.make_async_remote_copy(src_ref=src, dst_ref=dst, send_sem=send_sem.at[k], recv_sem=recv_sem.at[k],
                                          device_id=peer, device_id_type=MESH)
        cp.start()
        started.append(cp)
        return cp

    events = []

    def at(time, run):
        events.append((time, len(events), run))

    def aligned(start, count):
        return pl.ds(pl.multiple_of(start, 8), count)

    cp = {}

    def zg_start():
        cp["zg_up"] = copy(grad, grads.at[3, aligned(i * rows, rows)], z_up)
        cp["zg_dn"] = copy(grad, grads.at[1, aligned(i * rows, rows)], z_dn)

    def zg_forward():
        h = rows // 2
        first, second = aligned(i * rows, h), aligned(i * rows + h, h)
        cp["zg_up"].wait_recv()
        cp["zg_up2"] = copy(grads.at[3, first], grads.at[2, first], z_up)
        cp["zg_dn"].wait_recv()
        cp["zg_dn2"] = copy(grads.at[1, second], grads.at[2, second], z_dn)

    def zg_end():
        cp["zg_up2"].wait_recv()
        cp["zg_dn2"].wait_recv()

    def ring_start(key, piece_of, m, n, up, dn):
        cp[key, "up", 1] = copy(piece_of(m, 0), piece_of(m, 0), up)
        cp[key, "dn", 1] = copy(piece_of(m, 0), piece_of(m, 0), dn)

    def ring_step(key, step, piece_of, m, n, up, dn, arrived):
        last = n // 2
        lo, hi = lax.rem(m + n - step, n), lax.rem(m + step, n)
        nxt = step + 1
        cp[key, "up", step].wait_recv()
        if nxt <= last:
            part_no = 1 if nxt == last else 0
            cp[key, "up", nxt] = copy(piece_of(lo, part_no), piece_of(lo, part_no), up)
            if arrived:
                arrived(lo)
        cp[key, "dn", step].wait_recv()
        if nxt <= last:
            part_no = 2 if nxt == last else 0
            cp[key, "dn", nxt] = copy(piece_of(hi, part_no), piece_of(hi, part_no), dn)
            if arrived:
                arrived(hi)
        elif arrived:
            arrived(lo)

    def grad_rows(first, count, core_no):
        def piece_of(m, part_no):
            base = (2 * m + core_no) * rows
            h = rows // 2
            span = (aligned(base, rows), aligned(base, h), aligned(base + h, h))[part_no]
            return grads.at[pl.ds(first, count), span]
        return piece_of

    def core_copies(key, first, count):
        def arrived(m):
            ref = grad_rows(first, count, c)(m, 0)
            cp.setdefault((key, "core"), []).append(copy(ref, ref, core))
        return arrived

    ya = grad_rows(0, 1, c), y, n_y, yu, yd
    yb = grad_rows(1, n_tok - 1, c), y, n_y, yu, yd
    ya_core, yb_core = core_copies("ya", 0, 1), core_copies("yb", 1, n_tok - 1)

    def ya_start():
        grads[0, aligned(i * rows, rows), :] = grad[...]
        ring_start("ya", *ya)
        ya_core(y)

    def yb_start():
        ring_start("yb", *yb)
        yb_core(y)

    def cols_of(m, part_no):
        cut = 16
        span = (aligned(m * piece, piece), aligned(m * piece, cut), aligned(m * piece + cut, piece - cut))[part_no]
        return cols.at[pl.ds(1, n_tok - 1), span]

    xa = cols_of, x, n_x, xu, xd

    def acts_start():
        acts_t[...] = acts[...].T
        for d, peer in ((1, z_up), (3, z_dn), (2, z_op)):
            span = aligned(lax.rem(t + d, n_tok) * w_rows + x * piece, piece)
            cp["a2a", d] = copy(acts_t.at[span], cols.at[n_tok - d, aligned(x * piece, piece)], peer)

    def acts_split():
        acts_hi[...], acts_lo[...] = halves(acts_t[...])

    def xa_start():
        for d in (1, 3, 2):
            cp["a2a", d].wait_recv()
        ring_start("xa", *xa)

    def w_span(k):
        return pl.ds(k * quarter, quarter)

    def w_start():
        for ku, kd in ((0, 2), (1, 3), (2, 0), (3, 1)):
            cp["w_up", ku] = copy(weight.at[w_span(ku)], tile.at[t, w_span(ku)], z_up)
            cp["w_dn", kd] = copy(weight.at[w_span(kd)], tile.at[t, w_span(kd)], z_dn)
        tile[t] = weight[...]

    before, after, across = [lax.rem(t + d, n_tok) for d in (n_tok - 1, 1, 2)]

    def w_forward(k):
        cp["w_up", k].wait_recv()
        cp["w_up2", k] = copy(tile.at[before, w_span(k)], tile.at[before, w_span(k)], z_up)
        cp["w_dn", k + 2].wait_recv()
        cp["w_dn2", k + 2] = copy(tile.at[after, w_span(k + 2)], tile.at[after, w_span(k + 2)], z_dn)

    def w_near():
        for k in (2, 3):
            cp["w_up", k].wait_recv()
            cp["w_dn", k - 2].wait_recv()

    def w_far():
        for k in (0, 1):
            cp["w_up2", k].wait_recv()
            cp["w_dn2", k + 2].wait_recv()

    def out_term(block):
        span = pl.ds(pl.multiple_of(block * w_rows, 16), w_rows)
        return dot3((acts_hi[span], acts_lo[span]), halves(tile[block]), 0, 0)

    def out_store(value, add):
        for m in range(n_y):
            for k in range(2):
                rows_of = value[(2 * m + k) * rows:(2 * m + k + 1) * rows]
                part[k, m] = part[k, m] + rows_of if add else rows_of

    def out_near():
        out_store(out_term(t), False)
        out_store(out_term(before), True)
        out_store(out_term(after), True)

    def out_far():
        out_store(out_term(across), True)
        cp["pair"] = copy(part.at[1 - c], part_in, core)

    def scatter_start(key, dest, m, n, up, dn, slots):
        mid = lax.rem(m + n // 2, n)
        cp[key, "up", 0] = copy(dest(mid, 1), slots(0, 0, 1), up)
        cp[key, "dn", 0] = copy(dest(mid, 2), slots(1, 0, 2), dn)

    def scatter_step(key, step, dest, m, n, up, dn, slots):
        for way, peer in ((0, up), (1, dn)):
            name = ("up", "dn")[way]
            gap = n // 2 - step
            to = lax.rem(m + (gap if way == 0 else n - gap), n)
            part_no = (1 + way) if step == 1 else 0
            cp[key, name, step - 1].wait_recv()
            ref = dest(to, part_no)
            ref[...] = ref[...] + slots(way, step - 1, part_no)[...]
            cp[key, name, step] = copy(dest(to, 0), slots(way, step, 0), peer)

    def scatter_end(key, dest, m, n, up, dn, slots):
        last = n // 2 - 1
        cp[key, "up", last].wait_recv()
        cp[key, "dn", last].wait_recv()
        return dest(m, 0)[...] + slots(0, last, 0)[...] + slots(1, last, 0)[...]

    def out_dest(m, part_no):
        h = rows // 2
        return part.at[c, m, (pl.ds(0, rows), pl.ds(0, h), pl.ds(h, h))[part_no]]

    def out_slots(way, step, part_no):
        h = rows // 2
        return (y_up, y_dn)[way].at[step, (pl.ds(0, rows), pl.ds(0, h), pl.ds(h, h))[part_no]]

    yr = out_dest, y, n_y, yu, yd, out_slots

    def out_pair():
        cp["pair"].wait_recv()
        part[c] = part[c] + part_in[...]
        scatter_start("yr", *yr)

    def out_end():
        out[...] = scatter_end("yr", *yr)

    pair = t // 2

    def ga_of(k):
        def dest(m, part_no):
            return gpart.at[k, m, (pl.ds(0, 2), pl.ds(0, 1), pl.ds(1, 1))[part_no]]

        def slots(way, step, part_no):
            return (x_up, x_dn)[way].at[k, step, (pl.ds(0, 2), pl.ds(0, 1), pl.ds(1, 1))[part_no]]

        return dest, x, n_x, xu, xd, slots

    def ga_start(k):
        which = pair if k == 0 else 1 - pair
        blocks = tile[pl.ds(2 * which, 2)].reshape(2 * w_rows, weight.shape[1])
        value = dot3(halves(grads[0]), halves(blocks), 1, 1)
        for m in range(n_x):
            for z in range(2):
                gpart[k, m, z] = value[(z * n_x + m) * rows:(z * n_x + m + 1) * rows]
        scatter_start(("xr", k), *ga_of(k))

    def ga_swap(k):
        swap[k] = scatter_end(("xr", k), *ga_of(k))
        cp["zlo", k] = copy(swap.at[k, 1 - zl], swap_in.at[k], zlo)

    def ga_end():
        value = []
        for k in range(2):
            cp["zlo", k].wait_recv()
            value.append(swap[k, zl] + swap_in[k])
        width = value[0].shape[1]
        grad_acts[:, :width] = jnp.where(pair == 0, value[0], value[1])
        grad_acts[:, width:] = jnp.where(pair == 0, value[1], value[0])

    def wait_core(key):
        for copied in cp[key, "core"]:
            copied.wait_recv()

    def gw():
        own = pl.ds(pl.multiple_of(t * w_rows, 16), w_rows)
        total = dot3((acts_hi[own], acts_lo[own]), halves(grads[0]), 1, 0)
        for d in range(1, n_tok):
            total = total + dot3(halves(cols[d]), halves(grads[d]), 1, 0)
        grad_weight[...] = total

    at(0, zg_start)
    at(0.1, ya_start)
    at(0.2, acts_start)
    at(0.3, w_start)
    at(0.4, acts_split)
    at(4, zg_forward)
    at(5, lambda: ring_step("ya", 1, *ya, ya_core))
    at(7, xa_start)
    at(8, zg_end)
    at(8.1, yb_start)
    at(9, lambda: ring_step("ya", 2, *ya, ya_core))
    at(12, lambda: w_forward(0))
    at(13, lambda: ring_step("xa", 1, *xa, None))
    at(14, lambda: ring_step("ya", 3, *ya, ya_core))
    at(18, lambda: ring_step("ya", 4, *ya, ya_core))
    at(18.5, lambda: ring_step("xa", 2, *xa, None))
    at(19, lambda: w_forward(1))
    at(19.5, lambda: ring_step("yb", 1, *yb, yb_core))
    at(23, lambda: ring_step("xa", 3, *xa, None))
    at(26, lambda: ring_step("yb", 2, *yb, yb_core))
    at(26.5, lambda: ring_step("xa", 4, *xa, None))
    at(27, w_near)
    at(27.1, lambda: wait_core("ya"))
    at(27.2, lambda: ga_start(0))
    at(27.5, out_near)
    at(32, lambda: scatter_step(("xr", 0), 1, *ga_of(0)))
    at(34, lambda: ring_step("yb", 3, *yb, yb_core))
    at(36, lambda: scatter_step(("xr", 0), 2, *ga_of(0)))
    at(40, lambda: scatter_step(("xr", 0), 3, *ga_of(0)))
    at(41, lambda: ring_step("yb", 4, *yb, yb_core))
    at(44, lambda: ga_swap(0))
    at(45, w_far)
    at(45.1, out_far)
    at(45.2, lambda: ga_start(1))
    at(46, out_pair)
    at(46.5, lambda: wait_core("yb"))
    at(46.6, gw)
    for s in (1, 2, 3):
        at(46 + 4 * s, lambda s=s: scatter_step("yr", s, *yr))
        at(46.1 + 4 * s, lambda s=s: scatter_step(("xr", 1), s, *ga_of(1)))
    at(62, lambda: ga_swap(1))
    at(63, out_end)
    at(66, ga_end)
    for _, _, run in sorted(events, key=lambda event: event[:2]):
        run()
    for cp_started in started:
        cp_started.wait_send()


def shards(sizes, acts, weight, grad_out):
    n_tok, n_fin, n_fout = sizes
    n_y, n_x = n_fin // 2, n_fout // 2
    toks, depth = acts.shape
    w_rows, width = weight.shape
    rows = grad_out.shape[0]
    half = depth // 2
    vmem = pl.BlockSpec(memory_space=pltpu.VMEM)
    return pl.pallas_call(
        functools.partial(kernel, sizes),
        out_shape=(
            jax.ShapeDtypeStruct((rows, width), F32),
            jax.ShapeDtypeStruct((rows, depth), F32),
            jax.ShapeDtypeStruct((w_rows, width), F32),
        ),
        in_specs=[vmem] * 3,
        out_specs=(vmem,) * 3,
        scratch_shapes=[
            pltpu.VMEM((depth, toks), F32),
            pltpu.VMEM((depth, toks), jnp.bfloat16),
            pltpu.VMEM((depth, toks), jnp.bfloat16),
            pltpu.VMEM((n_tok, w_rows, toks), F32),
            pltpu.VMEM((n_tok, toks, width), F32),
            pltpu.VMEM((n_tok, w_rows, width), F32),
            pltpu.VMEM((2, n_y, rows, width), F32),
            pltpu.VMEM((n_y, rows, width), F32),
            pltpu.VMEM((n_y // 2, rows, width), F32),
            pltpu.VMEM((n_y // 2, rows, width), F32),
            pltpu.VMEM((2, n_x, 2, rows, half), F32),
            pltpu.VMEM((2, n_x // 2, 2, rows, half), F32),
            pltpu.VMEM((2, n_x // 2, 2, rows, half), F32),
            pltpu.VMEM((2, 2, rows, half), F32),
            pltpu.VMEM((2, rows, half), F32),
            pltpu.SemaphoreType.DMA((96,)),
            pltpu.SemaphoreType.DMA((96,)),
        ],
        compiler_params=pltpu.CompilerParams(collective_id=0, has_side_effects=True, vmem_limit_bytes=52 * 2**20),
    )(acts, weight, grad_out)


def solution(mesh):
    sizes = tuple(mesh.shape[name] for name in ("tok", "fin", "fout"))
    in_specs = (P("tok", "fin"), P(("fin", "tok"), "fout"), P(("tok", "fin"), "fout"))
    out_specs = (P(("tok", "fin"), "fout"), P(("tok", "fout"), "fin"), P(("fin", "tok"), "fout"))
    return jax.shard_map(functools.partial(shards, sizes), mesh=mesh, in_specs=in_specs, out_specs=out_specs, check_vma=False)
```

```python
import functools

import jax
import jax.numpy as jnp
from jax import lax
from jax.experimental import pallas as pl
from jax.experimental.pallas import tpu as pltpu
from jax.sharding import PartitionSpec as P

MESH = pl.DeviceIdType.MESH
F32 = jnp.float32

ORDER = (
    "zg0", "ya0", "a0", "w01", "w00", "yad1", "yad2", "zfd", "zfu", "w03", "yb0", "w02", "yau1", "xa0", "wfu1",
    "xad1", "yau2", "ybd1", "as", "yad3", "wfd1", "yc0", "xau1", "yau3", "ybu1", "ya4", "xau2", "yaw", "wfu0",
    "ybu2", "xad2", "wfd0", "ybd2", "wn", "xau3", "ycu1", "x00", "x0u1", "ycu2", "x0d1", "ycd1", "ybd3", "wfar",
    "pair", "g1", "x100", "ybu3", "x0d2", "ycu3", "yr00", "ycd2", "x10u1", "x10d1", "yb4", "x0u2", "yr0d1", "xad3",
    "yr0u1", "x10u2", "x10d2", "ycd3", "x0u3", "x0d3", "yr0d2", "yr0u2", "x10u3", "x10d3", "yc4", "ycw", "ybw",
    "yr0d3", "yr0u3", "xa4", "x04", "x104", "gw", "yr04", "end",
)


def halves(value):
    high = value.astype(jnp.bfloat16)
    return high, (value - high.astype(F32)).astype(jnp.bfloat16)


def dot3(left, right, left_dim, right_dim):
    dims = (((left_dim,), (right_dim,)), ((), ()))
    dot = functools.partial(lax.dot_general, dimension_numbers=dims, preferred_element_type=F32)
    return dot(left[0], right[0]) + (dot(left[0], right[1]) + dot(left[1], right[0]))


def kernel(sizes, acts_in, weight_in, grad_in, out, grad_acts, grad_weight,
           acts, acts_t, acts_hi, acts_lo, cols, grads, tile, part, part_in, y_up, y_dn, gpart, x_up, x_dn, swap, swap_in,
           send_sem, recv_sem, local_sem):
    n_tok, n_fin, n_fout = sizes
    n_y, n_x = n_fin // 2, n_fout // 2
    t, i, o = lax.axis_index("tok"), lax.axis_index("fin"), lax.axis_index("fout")
    y, c = i // 2, lax.rem(i, 2)
    zl, x = o // n_x, lax.rem(o, n_x)
    z_up, z_dn = [(lax.rem(t + d, n_tok), i, o) for d in (1, n_tok - 1)]
    yu, yd = [(t, lax.rem(i + d, n_fin), o) for d in (2, n_fin - 2)]
    core = (t, i + 1 - 2 * c, o)
    xu, xd = [(t, i, zl * n_x + lax.rem(x + d, n_x)) for d in (1, n_x - 1)]
    zlo = (t, i, lax.rem(o + n_x, n_fout))
    z_op = (lax.rem(t + 2, n_tok), i, lax.rem(o + n_x, n_fout))
    rows, w_rows = grad_in.shape[0], weight_in.shape[0]
    piece = w_rows // n_x
    quarter = w_rows // 4

    def aligned(start, count):
        return pl.ds(pl.multiple_of(start, 8), count)

    mine = aligned(i * rows, rows)
    loads = [
        pltpu.make_async_copy(grad_in, grads.at[0, mine], local_sem.at[0]),
        pltpu.make_async_copy(weight_in, tile.at[t], local_sem.at[1]),
        pltpu.make_async_copy(acts_in, acts, local_sem.at[2]),
    ]
    for load in loads:
        load.start()

    barrier = pltpu.get_barrier_semaphore()
    peers = (z_up, z_dn, z_op, yu, yd, core, xu, xd, zlo)
    for peer in peers:
        pl.semaphore_signal(barrier, inc=1, device_id=peer, device_id_type=MESH)
    pl.semaphore_wait(barrier, len(peers))
    for load in loads:
        load.wait()

    started = []
    cp = {}
    events = {}

    def copy(key, src, dst, peer):
        k = len(started)
        cp[key] = pltpu.make_async_remote_copy(src_ref=src, dst_ref=dst, send_sem=send_sem.at[k], recv_sem=recv_sem.at[k],
                                               device_id=peer, device_id_type=MESH)
        cp[key].start()
        started.append(cp[key])

    waited = set()

    def got(*keys):
        for key in keys:
            if key not in waited:
                waited.add(key)
                cp[key].wait_recv()

    def event(name):
        def add(run):
            events[name] = run
            return run
        return add


    h = rows // 2
    first, second = aligned(i * rows, h), aligned(i * rows + h, h)

    @event("zg0")
    def _():
        copy("zgu", grads.at[0, mine], grads.at[2, mine], z_up)
        copy("zgd", grads.at[0, mine], grads.at[1, mine], z_dn)

    @event("zfu")
    def _():
        got("zgu")
        copy("zgu2", grads.at[2, first], grads.at[3, first], z_up)

    @event("zfd")
    def _():
        got("zgd")
        copy("zgd2", grads.at[1, second], grads.at[3, second], z_dn)

    def gather(key, piece_of, m, n, up, dn, to_core, need):
        last = n // 2

        def begin():
            got(*need)
            copy(key + "u1", piece_of(m, 0), piece_of(m, 0), up)
            copy(key + "d1", piece_of(m, 0), piece_of(m, 0), dn)
            if to_core:
                copy(key + "c", piece_of(m, 0), piece_of(m, 0), core)

        def step(way, s):
            back = lax.rem(m + (n - s if way == "u" else s), n)
            got(f"{key}{way}{s}")
            k = 0 if s + 1 < last else (1 if way == "u" else 2)
            copy(f"{key}{way}{s + 1}", piece_of(back, k), piece_of(back, k), up if way == "u" else dn)
            if to_core:
                copy(f"{key}c{way}{s}", piece_of(back, 0), piece_of(back, 0), core)

        def finish():
            got(f"{key}u{last}", f"{key}d{last}")
            if to_core:
                back = lax.rem(m + last, n)
                copy(f"{key}c{last}", piece_of(back, 0), piece_of(back, 0), core)

        events[key + "0"] = begin
        for s in range(1, last):
            for way in "ud":
                events[f"{key}{way}{s}"] = functools.partial(step, way, s)
        events[f"{key}{last}"] = finish
        if to_core:
            inner = [f"{key}c{way}{s}" for s in range(1, last) for way in "ud"]
            events[key + "w"] = lambda: got(key + "c", *inner, f"{key}c{last}")

    def grad_rows(slots):
        def piece_of(m, k):
            base = (2 * m + c) * rows
            return grads.at[slots, (aligned(base, rows), aligned(base, h), aligned(base + h, h))[k]]
        return piece_of

    gather("ya", grad_rows(pl.ds(0, 1)), y, n_y, yu, yd, True, ())
    gather("yb", grad_rows(pl.ds(1, 2)), y, n_y, yu, yd, True, ())
    gather("yc", grad_rows(pl.ds(3, 1)), y, n_y, yu, yd, True, ("zgu2", "zgd2"))

    def cols_of(m, k):
        cut = 16
        base = m * piece
        return cols.at[pl.ds(1, n_tok - 1), (aligned(base, piece), aligned(base, cut), aligned(base + cut, piece - cut))[k]]

    gather("xa", cols_of, x, n_x, xu, xd, False, ("a1", "a3", "a2"))

    @event("a0")
    def _():
        acts_t[...] = acts[...].T
        for d, slot, peer in ((1, 2, z_up), (3, 1, z_dn), (2, 3, z_op)):
            span = aligned(lax.rem(t + d, n_tok) * w_rows + x * piece, piece)
            copy(f"a{d}", acts_t.at[span], cols.at[slot, aligned(x * piece, piece)], peer)

    @event("as")
    def _():
        acts_hi[...], acts_lo[...] = halves(acts_t[...])

    before, after, across = [lax.rem(t + d, n_tok) for d in (n_tok - 1, 1, 2)]

    def w_part(block, k):
        return tile.at[block, pl.ds(k * quarter, quarter)]

    def w_first(k):
        other = (k + 2) % 4
        copy(f"wu{k}", w_part(t, k), w_part(t, k), z_up)
        copy(f"wd{k}", w_part(t, other), w_part(t, other), z_dn)

    def w_up(k):
        got(f"wu{k}")
        copy(f"vu{k}", w_part(before, k), w_part(before, k), z_up)

    def w_dn(k):
        got(f"wd{k}")
        copy(f"vd{k}", w_part(after, k + 2), w_part(after, k + 2), z_dn)

    for k in range(4):
        events[f"w0{k}"] = functools.partial(w_first, k)
    for k in range(2):
        events[f"wfu{k}"] = functools.partial(w_up, k)
        events[f"wfd{k}"] = functools.partial(w_dn, k)

    def out_add(blocks, add):
        value = None
        for block in blocks:
            span = pl.ds(pl.multiple_of(block * w_rows, 16), w_rows)
            term = dot3((acts_hi[span], acts_lo[span]), halves(tile[block]), 0, 0)
            value = term if value is None else value + term
        for m in range(n_y):
            for k in range(2):
                rows_of = value[(2 * m + k) * rows:(2 * m + k + 1) * rows]
                part[k, m] = part[k, m] + rows_of if add else rows_of

    @event("wn")
    def _():
        got(*[f"w{way}{k}" for way in "ud" for k in range(4)])
        out_add((t, before, after), False)

    @event("wfar")
    def _():
        got("vu0", "vu1", "vd0", "vd1")
        out_add((across,), True)

    @event("pair")
    def _():
        copy("pair", part.at[1 - c], part_in, core)

    def scatter(key, dest, slots, m, n, up, dn, ready, done):
        last = n // 2 - 1

        def begin():
            ready()
            mid = lax.rem(m + n // 2, n)
            copy(key + "u0", dest(mid, 1), slots(0, 0, 1), up)
            copy(key + "d0", dest(mid, 2), slots(1, 0, 2), dn)

        def step(way, s):
            gap = n // 2 - s
            to = lax.rem(m + (n - gap if way else gap), n)
            k = 1 + way if s == 1 else 0
            name = "ud"[way]
            got(f"{key}{name}{s - 1}")
            dest(to, k)[...] = dest(to, k)[...] + slots(way, s - 1, k)[...]
            copy(f"{key}{name}{s}", dest(to, 0), slots(way, s, 0), dn if way else up)

        def finish():
            got(f"{key}u{last}", f"{key}d{last}")
            done(dest(m, 0)[...] + slots(0, last, 0)[...] + slots(1, last, 0)[...])

        events[key + "0"] = begin
        for s in range(1, last + 1):
            for way in range(2):
                events[f"{key}{'ud'[way]}{s}"] = functools.partial(step, way, s)
        events[f"{key}{last + 1}"] = finish

    row_parts = (pl.ds(0, rows), pl.ds(0, h), pl.ds(h, h))

    def out_ready():
        got("pair")
        part[c] = part[c] + part_in[...]

    def out_done(value):
        out[...] = value

    scatter("yr0", lambda m, k: part.at[c, m, row_parts[k]], lambda way, s, k: (y_up, y_dn)[way].at[s, row_parts[k]],
            y, n_y, yu, yd, out_ready, out_done)

    pair = t // 2
    zlo_parts = (pl.ds(0, 2), pl.ds(0, 1), pl.ds(1, 1))

    def ga_compute(k):
        which = 1 - pair if k else pair
        blocks = tile[pl.ds(2 * which, 2)].reshape(2 * w_rows, weight_in.shape[1])
        value = dot3(halves(grads[0]), halves(blocks), 1, 1)
        for m in range(n_x):
            for z in range(2):
                gpart[k, m, z] = value[(z * n_x + m) * rows:(z * n_x + m + 1) * rows]

    def ga_scatter(key, k, ready):
        def done(value):
            swap[k] = value
            copy(f"l{k}", swap.at[k, 1 - zl], swap_in.at[k], zlo)

        scatter(key, lambda m, j: gpart.at[k, m, zlo_parts[j]], lambda way, s, j: (x_up, x_dn)[way].at[k, s, zlo_parts[j]],
                x, n_x, xu, xd, ready, done)

    ga_scatter("x0", 0, functools.partial(ga_compute, 0))
    events["g1"] = functools.partial(ga_compute, 1)
    ga_scatter("x10", 1, lambda: None)

    @event("gw")
    def _():
        own = pl.ds(pl.multiple_of(t * w_rows, 16), w_rows)
        total = dot3((acts_hi[own], acts_lo[own]), halves(grads[0]), 1, 0)
        for slot in range(1, n_tok):
            total = total + dot3(halves(cols[slot]), halves(grads[slot]), 1, 0)
        grad_weight[...] = total

    @event("end")
    def _():
        got("l0", "l1")
        value = [swap[k, zl] + swap_in[k] for k in range(2)]
        width = value[0].shape[1]
        grad_acts[:, :width] = jnp.where(pair == 0, value[0], value[1])
        grad_acts[:, width:] = jnp.where(pair == 0, value[1], value[0])

    for name in ORDER:
        events.pop(name)()
    assert not events
    for sent in started:
        sent.wait_send()


def shards(sizes, acts, weight, grad_out):
    n_tok, n_fin, n_fout = sizes
    n_y, n_x = n_fin // 2, n_fout // 2
    toks, depth = acts.shape
    w_rows, width = weight.shape
    rows = grad_out.shape[0]
    half = depth // 2
    vmem = pl.BlockSpec(memory_space=pltpu.VMEM)
    return pl.pallas_call(
        functools.partial(kernel, sizes),
        out_shape=(
            jax.ShapeDtypeStruct((rows, width), F32),
            jax.ShapeDtypeStruct((rows, depth), F32),
            jax.ShapeDtypeStruct((w_rows, width), F32),
        ),
        in_specs=[pl.BlockSpec(memory_space=pl.ANY)] * 3,
        out_specs=(vmem,) * 3,
        scratch_shapes=[
            pltpu.VMEM((toks, depth), F32),
            pltpu.VMEM((depth, toks), F32),
            pltpu.VMEM((depth, toks), jnp.bfloat16),
            pltpu.VMEM((depth, toks), jnp.bfloat16),
            pltpu.VMEM((n_tok, w_rows, toks), F32),
            pltpu.VMEM((n_tok, toks, width), F32),
            pltpu.VMEM((n_tok, w_rows, width), F32),
            pltpu.VMEM((2, n_y, rows, width), F32),
            pltpu.VMEM((n_y, rows, width), F32),
            pltpu.VMEM((n_y // 2, rows, width), F32),
            pltpu.VMEM((n_y // 2, rows, width), F32),
            pltpu.VMEM((2, n_x, 2, rows, half), F32),
            pltpu.VMEM((2, n_x // 2, 2, rows, half), F32),
            pltpu.VMEM((2, n_x // 2, 2, rows, half), F32),
            pltpu.VMEM((2, 2, rows, half), F32),
            pltpu.VMEM((2, rows, half), F32),
            pltpu.SemaphoreType.DMA((112,)),
            pltpu.SemaphoreType.DMA((112,)),
            pltpu.SemaphoreType.DMA((3,)),
        ],
        compiler_params=pltpu.CompilerParams(collective_id=0, has_side_effects=True, vmem_limit_bytes=54 * 2**20),
    )(acts, weight, grad_out)


def solution(mesh):
    sizes = tuple(mesh.shape[name] for name in ("tok", "fin", "fout"))
    in_specs = (P("tok", "fin"), P(("fin", "tok"), "fout"), P(("tok", "fin"), "fout"))
    out_specs = (P(("tok", "fin"), "fout"), P(("tok", "fout"), "fin"), P(("fin", "tok"), "fout"))
    return jax.shard_map(functools.partial(shards, sizes), mesh=mesh, in_specs=in_specs, out_specs=out_specs, check_vma=False)
```

```python
import functools

import jax
import jax.numpy as jnp
from jax import lax
from jax.experimental import pallas as pl
from jax.experimental.pallas import tpu as pltpu
from jax.sharding import PartitionSpec as P

MESH = pl.DeviceIdType.MESH
F32 = jnp.float32

ORDER = (
    "w01", "zg0", "ya0", "yad1", "a0", "zfu", "w00", "yau1", "yad2", "yau2", "yad3", "zfd", "w03", "w02", "xa0",
    "yb0", "xau1", "yau3", "ybd1", "yc0", "ybu1", "xad1", "wfu0", "xau2", "ya4", "as", "ycu1", "wfd0", "xau3",
    "ybd2", "ybu2", "wfu1", "xad2", "yaw", "wn", "wfd1", "ycd1", "x00", "wfar0", "ycd2", "xad3", "x0u1", "x0d1",
    "yr00", "ybu3", "ycd3", "xa4", "wfar1", "g1", "x100", "x0u2", "x0d2", "yr10", "ycu2", "ybd3", "x10u1", "x10d1",
    "yr0d1", "yr0u1", "ycu3", "yr1u1", "yr1d1", "x10u2", "x10d2", "yr0u2", "x0u3", "yb4", "x0d3", "yr0d2", "yr1d2",
    "yr1u2", "x10u3", "x10d3", "yc4", "yr0d3", "yr0u3", "yr1d3", "x04", "yr1u3", "x104", "ycw", "ybw", "gw", "yr04",
    "yr14", "end",
)


def halves(value):
    high = value.astype(jnp.bfloat16)
    return high, (value - high.astype(F32)).astype(jnp.bfloat16)


def dot3(left, right, left_dim, right_dim):
    dims = (((left_dim,), (right_dim,)), ((), ()))
    dot = functools.partial(lax.dot_general, dimension_numbers=dims, preferred_element_type=F32)
    return dot(left[0], right[0]) + (dot(left[0], right[1]) + dot(left[1], right[0]))


def kernel(sizes, acts_in, weight_in, grad_in, out, grad_acts, grad_weight,
           acts, acts_t, acts_hi, acts_lo, cols, grads, tile, part, part_in, y_up, y_dn, early, late, send_sem, recv_sem, local_sem):
    n_tok, n_fin, n_fout = sizes
    n_y, n_x = n_fin // 2, n_fout // 2
    t, i, o = lax.axis_index("tok"), lax.axis_index("fin"), lax.axis_index("fout")
    y, c = i // 2, lax.rem(i, 2)
    zl, x = o // n_x, lax.rem(o, n_x)
    z_up, z_dn = [(lax.rem(t + d, n_tok), i, o) for d in (1, n_tok - 1)]
    yu, yd = [(t, lax.rem(i + d, n_fin), o) for d in (2, n_fin - 2)]
    core = (t, i + 1 - 2 * c, o)
    xu, xd = [(t, i, zl * n_x + lax.rem(x + d, n_x)) for d in (1, n_x - 1)]
    zlo = (t, i, lax.rem(o + n_x, n_fout))
    z_op = (lax.rem(t + 2, n_tok), i, lax.rem(o + n_x, n_fout))
    rows, w_rows = grad_in.shape[0], weight_in.shape[0]
    piece = w_rows // n_x
    depth, width = acts_in.shape[1], weight_in.shape[1]
    lanes = width // 2
    w_half = w_rows // 2

    def aligned(start, count):
        return pl.ds(pl.multiple_of(start, 8), count)

    mine = aligned(i * rows, rows)
    loads = [
        pltpu.make_async_copy(grad_in, grads.at[0, mine], local_sem.at[0]),
        pltpu.make_async_copy(weight_in, tile.at[aligned(t * w_rows, w_rows)], local_sem.at[1]),
        pltpu.make_async_copy(acts_in, acts, local_sem.at[2]),
    ]
    for load in loads:
        load.start()

    barrier = pltpu.get_barrier_semaphore()
    peers = (z_up, z_dn, z_op, yu, yd, core, xu, xd, zlo)
    for peer in peers:
        pl.semaphore_signal(barrier, inc=1, device_id=peer, device_id_type=MESH)
    pl.semaphore_wait(barrier, len(peers))
    for load in loads:
        load.wait()

    started = []
    cp = {}
    events = {}

    def copy(key, src, dst, peer):
        k = len(started)
        cp[key] = pltpu.make_async_remote_copy(src_ref=src, dst_ref=dst, send_sem=send_sem.at[k], recv_sem=recv_sem.at[k],
                                               device_id=peer, device_id_type=MESH)
        cp[key].start()
        started.append(cp[key])

    waited = set()

    def got(*keys):
        for key in keys:
            if key not in waited:
                waited.add(key)
                cp[key].wait_recv()

    def event(name):
        def add(run):
            events[name] = run
            return run
        return add


    h = rows // 2
    first, second = aligned(i * rows, h), aligned(i * rows + h, h)

    @event("zg0")
    def _():
        copy("zgu", grads.at[0, mine], grads.at[2, mine], z_up)
        copy("zgd", grads.at[0, mine], grads.at[1, mine], z_dn)

    @event("zfu")
    def _():
        got("zgu")
        copy("zgu2", grads.at[2, first], grads.at[3, first], z_up)

    @event("zfd")
    def _():
        got("zgd")
        copy("zgd2", grads.at[1, second], grads.at[3, second], z_dn)

    def gather(key, piece_of, m, n, up, dn, to_core, need):
        last = n // 2

        def begin():
            got(*need)
            copy(key + "u1", piece_of(m, 0), piece_of(m, 0), up)
            copy(key + "d1", piece_of(m, 0), piece_of(m, 0), dn)
            if to_core:
                copy(key + "c", piece_of(m, 0), piece_of(m, 0), core)

        def step(way, s):
            back = lax.rem(m + (n - s if way == "u" else s), n)
            got(f"{key}{way}{s}")
            k = 0 if s + 1 < last else (1 if way == "u" else 2)
            copy(f"{key}{way}{s + 1}", piece_of(back, k), piece_of(back, k), up if way == "u" else dn)
            if to_core:
                copy(f"{key}c{way}{s}", piece_of(back, 0), piece_of(back, 0), core)

        def finish():
            got(f"{key}u{last}", f"{key}d{last}")
            if to_core:
                back = lax.rem(m + last, n)
                copy(f"{key}c{last}", piece_of(back, 0), piece_of(back, 0), core)

        events[key + "0"] = begin
        for s in range(1, last):
            for way in "ud":
                events[f"{key}{way}{s}"] = functools.partial(step, way, s)
        events[f"{key}{last}"] = finish
        if to_core:
            inner = [f"{key}c{way}{s}" for s in range(1, last) for way in "ud"]
            events[key + "w"] = lambda: got(key + "c", *inner, f"{key}c{last}")

    def grad_rows(slots):
        def piece_of(m, k):
            base = (2 * m + c) * rows
            return grads.at[slots, (aligned(base, rows), aligned(base, h), aligned(base + h, h))[k]]
        return piece_of

    gather("ya", grad_rows(pl.ds(0, 1)), y, n_y, yu, yd, True, ())
    gather("yb", grad_rows(pl.ds(1, 2)), y, n_y, yu, yd, True, ())
    gather("yc", grad_rows(pl.ds(3, 1)), y, n_y, yu, yd, True, ("zgu2", "zgd2"))

    def cols_of(m, k):
        cut = 16
        base = m * piece
        return cols.at[pl.ds(1, n_tok - 1), (aligned(base, piece), aligned(base, cut), aligned(base + cut, piece - cut))[k]]

    gather("xa", cols_of, x, n_x, xu, xd, False, ("a1", "a3", "a2"))

    @event("a0")
    def _():
        acts_t[...] = acts[...].T
        for d, slot, peer in ((1, 2, z_up), (3, 1, z_dn), (2, 3, z_op)):
            span = aligned(lax.rem(t + d, n_tok) * w_rows + x * piece, piece)
            copy(f"a{d}", acts_t.at[span], cols.at[slot, aligned(x * piece, piece)], peer)

    @event("as")
    def _():
        acts_hi[...], acts_lo[...] = halves(acts_t[...])

    before, after, across = [lax.rem(t + d, n_tok) for d in (n_tok - 1, 1, 2)]

    def w_part(block, k):
        return tile.at[aligned(block * w_rows + k // 2 * w_half, w_half), pl.ds(k % 2 * lanes, lanes)]

    def w_first(k):
        other = (k + 2) % 4
        copy(f"wu{k}", w_part(t, k), w_part(t, k), z_up)
        copy(f"wd{k}", w_part(t, other), w_part(t, other), z_dn)

    def w_up(k):
        got(f"wu{k}")
        copy(f"vu{k}", w_part(before, k), w_part(before, k), z_up)

    def w_dn(k):
        got(f"wd{k}")
        copy(f"vd{k}", w_part(after, k + 2), w_part(after, k + 2), z_dn)

    for k in range(4):
        events[f"w0{k}"] = functools.partial(w_first, k)
    for k in range(2):
        events[f"wfu{k}"] = functools.partial(w_up, k)
        events[f"wfd{k}"] = functools.partial(w_dn, k)

    def out_term(block, columns):
        span = pl.ds(pl.multiple_of(block * w_rows, 16), w_rows)
        return dot3((acts_hi[span], acts_lo[span]), halves(tile[aligned(block * w_rows, w_rows), columns]), 0, 0)

    def out_rows(value, m, k):
        return value[(2 * m + k) * rows:(2 * m + k + 1) * rows]

    @event("wn")
    def _():
        got(*[f"w{way}{k}" for way in "ud" for k in range(4)])
        value = out_term(t, pl.ds(0, width)) + out_term(before, pl.ds(0, width)) + out_term(after, pl.ds(0, width))
        for j in range(2):
            for m in range(n_y):
                for k in range(2):
                    part[j, k, m] = out_rows(value, m, k)[:, j * lanes:(j + 1) * lanes]

    def out_far(j):
        got(f"vu{j}", f"vd{j}")
        value = out_term(across, pl.ds(j * lanes, lanes))
        for k in range(2):
            for m in range(n_y):
                part[j, k, m] = part[j, k, m] + out_rows(value, m, k)
        copy(f"pair{j}", part.at[j, 1 - c], part_in.at[j], core)

    for j in range(2):
        events[f"wfar{j}"] = functools.partial(out_far, j)

    def scatter(key, dest, slots, m, n, up, dn, ready, done):
        last = n // 2 - 1

        def begin():
            ready()
            mid = lax.rem(m + n // 2, n)
            copy(key + "u0", dest(mid, 1), slots(0, 0, 1), up)
            copy(key + "d0", dest(mid, 2), slots(1, 0, 2), dn)

        def step(way, s):
            gap = n // 2 - s
            to = lax.rem(m + (n - gap if way else gap), n)
            k = 1 + way if s == 1 else 0
            name = "ud"[way]
            got(f"{key}{name}{s - 1}")
            dest(to, k)[...] = dest(to, k)[...] + slots(way, s - 1, k)[...]
            copy(f"{key}{name}{s}", dest(to, 0), slots(way, s, 0), dn if way else up)

        def finish():
            got(f"{key}u{last}", f"{key}d{last}")
            done(dest(m, 0)[...] + slots(0, last, 0)[...] + slots(1, last, 0)[...])

        events[key + "0"] = begin
        for s in range(1, last + 1):
            for way in range(2):
                events[f"{key}{'ud'[way]}{s}"] = functools.partial(step, way, s)
        events[f"{key}{last + 1}"] = finish

    row_parts = (pl.ds(0, rows), pl.ds(0, h), pl.ds(h, h))

    def out_ready(j):
        got(f"pair{j}")
        part[j, c] = part[j, c] + part_in[j]

    def out_done(j, value):
        out[:, j * lanes:(j + 1) * lanes] = value

    def out_scatter(j):
        scatter(f"yr{j}", lambda m, k: part.at[j, c, m, row_parts[k]], lambda way, s, k: (y_up, y_dn)[way].at[j, s, row_parts[k]],
                y, n_y, yu, yd, functools.partial(out_ready, j), functools.partial(out_done, j))

    out_scatter(0)
    out_scatter(1)

    pair, odd = t // 2, lax.rem(t, 2)
    unit = depth // 6
    own_at, other_at = pair * 3 * unit, (1 - pair) * 3 * unit
    first_at, last_at = other_at + 2 * unit * (1 - odd), other_at + unit * odd
    zlo_parts = (pl.ds(0, 2), pl.ds(0, 1), pl.ds(1, 1))

    def ga_store(buffer, blocks):
        value = dot3(halves(grads[0]), halves(blocks), 1, 1)
        for m in range(n_x):
            for z in range(2):
                buffer[m, z] = value[(z * n_x + m) * rows:(z * n_x + m + 1) * rows]

    def ga_early():
        ga_store(early[0], jnp.concatenate([tile[aligned(own_at, 3 * unit)], tile[aligned(first_at, unit)]], 0))

    def ga_late():
        ga_store(late[0], tile[aligned(last_at, 2 * unit)])

    def ga_scatter(key, swapped, buffers, ready):
        buffer, up_in, dn_in, swap, swap_in = buffers

        def done(value):
            swap[...] = value
            copy(swapped, swap.at[1 - zl], swap_in, zlo)

        scatter(key, lambda m, j: buffer.at[m, zlo_parts[j]], lambda way, s, j: (up_in, dn_in)[way].at[s, zlo_parts[j]],
                x, n_x, xu, xd, ready, done)

    ga_scatter("x0", "l0", early, ga_early)
    events["g1"] = ga_late
    ga_scatter("x10", "l1", late, lambda: None)

    @event("gw")
    def _():
        own = pl.ds(pl.multiple_of(t * w_rows, 16), w_rows)
        total = dot3((acts_hi[own], acts_lo[own]), halves(grads[0]), 1, 0)
        for slot in range(1, n_tok):
            total = total + dot3(halves(cols[slot]), halves(grads[slot]), 1, 0)
        grad_weight[...] = total

    def columns(start, count):
        return pl.ds(pl.multiple_of(start, unit), count)

    @event("end")
    def _():
        got("l0")
        value = early[3][zl] + early[4][...]
        grad_acts[:, columns(own_at, 3 * unit)] = value[:, :3 * unit]
        grad_acts[:, columns(first_at, unit)] = value[:, 3 * unit:]
        got("l1")
        grad_acts[:, columns(last_at, 2 * unit)] = late[3][zl] + late[4][...]

    for name in ORDER:
        events.pop(name)()
    assert not events
    for sent in started:
        sent.wait_send()


def shards(sizes, acts, weight, grad_out):
    n_tok, n_fin, n_fout = sizes
    n_y, n_x = n_fin // 2, n_fout // 2
    toks, depth = acts.shape
    w_rows, width = weight.shape
    rows = grad_out.shape[0]
    unit = depth // 6

    def scattered(count):
        shapes = [(n_x, 2), (n_x // 2, 2), (n_x // 2, 2), (2,), ()]
        return [pltpu.VMEM((*shape, rows, count), F32) for shape in shapes]

    vmem = pl.BlockSpec(memory_space=pltpu.VMEM)
    return pl.pallas_call(
        functools.partial(kernel, sizes),
        out_shape=(
            jax.ShapeDtypeStruct((rows, width), F32),
            jax.ShapeDtypeStruct((rows, depth), F32),
            jax.ShapeDtypeStruct((w_rows, width), F32),
        ),
        in_specs=[pl.BlockSpec(memory_space=pl.ANY)] * 3,
        out_specs=(vmem,) * 3,
        scratch_shapes=[
            pltpu.VMEM((toks, depth), F32),
            pltpu.VMEM((depth, toks), F32),
            pltpu.VMEM((depth, toks), jnp.bfloat16),
            pltpu.VMEM((depth, toks), jnp.bfloat16),
            pltpu.VMEM((n_tok, w_rows, toks), F32),
            pltpu.VMEM((n_tok, toks, width), F32),
            pltpu.VMEM((n_tok * w_rows, width), F32),
            pltpu.VMEM((2, 2, n_y, rows, width // 2), F32),
            pltpu.VMEM((2, n_y, rows, width // 2), F32),
            pltpu.VMEM((2, n_y // 2, rows, width // 2), F32),
            pltpu.VMEM((2, n_y // 2, rows, width // 2), F32),
            scattered(4 * unit),
            scattered(2 * unit),
            pltpu.SemaphoreType.DMA((128,)),
            pltpu.SemaphoreType.DMA((128,)),
            pltpu.SemaphoreType.DMA((3,)),
        ],
        compiler_params=pltpu.CompilerParams(collective_id=0, has_side_effects=True, vmem_limit_bytes=54 * 2**20),
    )(acts, weight, grad_out)


def solution(mesh):
    sizes = tuple(mesh.shape[name] for name in ("tok", "fin", "fout"))
    in_specs = (P("tok", "fin"), P(("fin", "tok"), "fout"), P(("tok", "fin"), "fout"))
    out_specs = (P(("tok", "fin"), "fout"), P(("tok", "fout"), "fin"), P(("fin", "tok"), "fout"))
    return jax.shard_map(functools.partial(shards, sizes), mesh=mesh, in_specs=in_specs, out_specs=out_specs, check_vma=False)
```

```python
import functools

import jax
import jax.numpy as jnp
from jax import lax
from jax.experimental import pallas as pl
from jax.experimental.pallas import tpu as pltpu
from jax.sharding import PartitionSpec as P

MESH = pl.DeviceIdType.MESH
F32 = jnp.float32

ORDER = (
    "zg0", "ya0", "a0", "yad1", "yau1", "w03", "yad2", "w01", "zfd", "yau2", "w00", "yad3", "zfu", "xa0", "yb0",
    "yau3", "xad1", "as", "ybu1", "ya4", "yc0", "xau1", "ybd1", "w02", "xad2", "ycu1", "wfu0", "ycd1", "yaw",
    "xau2", "ybd2", "ybu2", "xad3", "wfu1", "wfd0", "ycu2", "wn", "wfd1", "xau3", "x00", "ycu3", "ycd2", "wfar0",
    "gwa", "ybd3", "x0u1", "x0d1", "yr00", "ycd3", "wfar1", "g1", "x100", "x0u2", "x0d2", "yr0u1", "yr10", "yr0d1",
    "x10u1", "x10d1", "ybu3", "yc4", "yr1u1", "yr1d1", "yr0u2", "x10u2", "x10d2", "yr0d2", "x0u3", "x0d3", "yr1d2",
    "yr1u2", "yb4", "x10u3", "x10d3", "yr0u3", "yr0d3", "yr1d3", "x04", "yr1u3", "xa4", "x104", "ybw", "gwb", "ycw",
    "gwc", "yr04", "yr14", "end",
)


def halves(value):
    high = value.astype(jnp.bfloat16)
    return high, (value - high.astype(F32)).astype(jnp.bfloat16)


def dot3(left, right, left_dim, right_dim):
    dims = (((left_dim,), (right_dim,)), ((), ()))
    dot = functools.partial(lax.dot_general, dimension_numbers=dims, preferred_element_type=F32)
    return dot(left[0], right[0]) + (dot(left[0], right[1]) + dot(left[1], right[0]))


def kernel(sizes, acts_in, weight_in, grad_in, out, grad_acts, grad_weight,
           acts, acts_t, acts_hi, acts_lo, cols, grads, tile, part, part_in, y_up, y_dn, early, late, send_sem, recv_sem, local_sem):
    n_tok, n_fin, n_fout = sizes
    n_y, n_x = n_fin // 2, n_fout // 2
    t, i, o = lax.axis_index("tok"), lax.axis_index("fin"), lax.axis_index("fout")
    y, c = i // 2, lax.rem(i, 2)
    zl, x = o // n_x, lax.rem(o, n_x)
    z_up, z_dn = [(lax.rem(t + d, n_tok), i, o) for d in (1, n_tok - 1)]
    yu, yd = [(t, lax.rem(i + d, n_fin), o) for d in (2, n_fin - 2)]
    core = (t, i + 1 - 2 * c, o)
    xu, xd = [(t, i, zl * n_x + lax.rem(x + d, n_x)) for d in (1, n_x - 1)]
    zlo = (t, i, lax.rem(o + n_x, n_fout))
    z_op = (lax.rem(t + 2, n_tok), i, lax.rem(o + n_x, n_fout))
    rows, w_rows = grad_in.shape[0], weight_in.shape[0]
    piece = w_rows // n_x
    depth, width = acts_in.shape[1], weight_in.shape[1]
    lanes = width // 2
    w_half = w_rows // 2

    def aligned(start, count):
        return pl.ds(pl.multiple_of(start, 8), count)

    mine = aligned(i * rows, rows)
    loads = [
        pltpu.make_async_copy(grad_in, grads.at[0, mine], local_sem.at[0]),
        pltpu.make_async_copy(weight_in, tile.at[aligned(t * w_rows, w_rows)], local_sem.at[1]),
        pltpu.make_async_copy(acts_in, acts, local_sem.at[2]),
    ]
    for load in loads:
        load.start()

    barrier = pltpu.get_barrier_semaphore()
    peers = (z_up, z_dn, z_op, yu, yd, core, xu, xd, zlo)
    for peer in peers:
        pl.semaphore_signal(barrier, inc=1, device_id=peer, device_id_type=MESH)
    pl.semaphore_wait(barrier, len(peers))
    for load in loads:
        load.wait()

    started = []
    cp = {}
    events = {}

    def copy(key, src, dst, peer):
        k = len(started)
        cp[key] = pltpu.make_async_remote_copy(src_ref=src, dst_ref=dst, send_sem=send_sem.at[k], recv_sem=recv_sem.at[k],
                                               device_id=peer, device_id_type=MESH)
        cp[key].start()
        started.append(cp[key])

    waited = set()

    def got(*keys):
        for key in keys:
            if key not in waited:
                waited.add(key)
                cp[key].wait_recv()

    def event(name):
        def add(run):
            events[name] = run
            return run
        return add


    h = rows // 2
    first, second = aligned(i * rows, h), aligned(i * rows + h, h)

    @event("zg0")
    def _():
        copy("zgu", grads.at[0, mine], grads.at[2, mine], z_up)
        copy("zgd", grads.at[0, mine], grads.at[1, mine], z_dn)

    @event("zfu")
    def _():
        got("zgu")
        copy("zgu2", grads.at[2, first], grads.at[3, first], z_up)

    @event("zfd")
    def _():
        got("zgd")
        copy("zgd2", grads.at[1, second], grads.at[3, second], z_dn)

    def gather(key, piece_of, m, n, up, dn, to_core, need):
        last = n // 2

        def begin():
            got(*need)
            copy(key + "u1", piece_of(m, 0), piece_of(m, 0), up)
            copy(key + "d1", piece_of(m, 0), piece_of(m, 0), dn)
            if to_core:
                copy(key + "c", piece_of(m, 0), piece_of(m, 0), core)

        def step(way, s):
            back = lax.rem(m + (n - s if way == "u" else s), n)
            got(f"{key}{way}{s}")
            k = 0 if s + 1 < last else (1 if way == "u" else 2)
            copy(f"{key}{way}{s + 1}", piece_of(back, k), piece_of(back, k), up if way == "u" else dn)
            if to_core:
                copy(f"{key}c{way}{s}", piece_of(back, 0), piece_of(back, 0), core)

        def finish():
            got(f"{key}u{last}", f"{key}d{last}")
            if to_core:
                back = lax.rem(m + last, n)
                copy(f"{key}c{last}", piece_of(back, 0), piece_of(back, 0), core)

        events[key + "0"] = begin
        for s in range(1, last):
            for way in "ud":
                events[f"{key}{way}{s}"] = functools.partial(step, way, s)
        events[f"{key}{last}"] = finish
        if to_core:
            inner = [f"{key}c{way}{s}" for s in range(1, last) for way in "ud"]
            events[key + "w"] = lambda: got(key + "c", *inner, f"{key}c{last}")

    def grad_rows(slots):
        def piece_of(m, k):
            base = (2 * m + c) * rows
            return grads.at[slots, (aligned(base, rows), aligned(base, h), aligned(base + h, h))[k]]
        return piece_of

    gather("ya", grad_rows(pl.ds(0, 1)), y, n_y, yu, yd, True, ())
    gather("yb", grad_rows(pl.ds(1, 2)), y, n_y, yu, yd, True, ())
    gather("yc", grad_rows(pl.ds(3, 1)), y, n_y, yu, yd, True, ("zgu2", "zgd2"))

    def cols_of(m, k):
        cut = 16
        base = m * piece
        return cols.at[pl.ds(1, n_tok - 1), (aligned(base, piece), aligned(base, cut), aligned(base + cut, piece - cut))[k]]

    gather("xa", cols_of, x, n_x, xu, xd, False, ("a1", "a3", "a2"))

    @event("a0")
    def _():
        acts_t[...] = acts[...].T
        for d, slot, peer in ((1, 2, z_up), (3, 1, z_dn), (2, 3, z_op)):
            span = aligned(lax.rem(t + d, n_tok) * w_rows + x * piece, piece)
            copy(f"a{d}", acts_t.at[span], cols.at[slot, aligned(x * piece, piece)], peer)

    @event("as")
    def _():
        acts_hi[...], acts_lo[...] = halves(acts_t[...])

    before, after, across = [lax.rem(t + d, n_tok) for d in (n_tok - 1, 1, 2)]

    def w_part(block, k):
        return tile.at[aligned(block * w_rows + k // 2 * w_half, w_half), pl.ds(k % 2 * lanes, lanes)]

    def w_first(k):
        other = (k + 2) % 4
        copy(f"wu{k}", w_part(t, k), w_part(t, k), z_up)
        copy(f"wd{k}", w_part(t, other), w_part(t, other), z_dn)

    def w_up(k):
        got(f"wu{k}")
        copy(f"vu{k}", w_part(before, k), w_part(before, k), z_up)

    def w_dn(k):
        got(f"wd{k}")
        copy(f"vd{k}", w_part(after, k + 2), w_part(after, k + 2), z_dn)

    for k in range(4):
        events[f"w0{k}"] = functools.partial(w_first, k)
    for k in range(2):
        events[f"wfu{k}"] = functools.partial(w_up, k)
        events[f"wfd{k}"] = functools.partial(w_dn, k)

    def out_term(block, columns):
        span = pl.ds(pl.multiple_of(block * w_rows, 16), w_rows)
        return dot3((acts_hi[span], acts_lo[span]), halves(tile[aligned(block * w_rows, w_rows), columns]), 0, 0)

    def out_rows(value, m, k):
        return value[(2 * m + k) * rows:(2 * m + k + 1) * rows]

    @event("wn")
    def _():
        got(*[f"w{way}{k}" for way in "ud" for k in range(4)])
        value = out_term(t, pl.ds(0, width)) + out_term(before, pl.ds(0, width)) + out_term(after, pl.ds(0, width))
        for j in range(2):
            for m in range(n_y):
                for k in range(2):
                    part[j, k, m] = out_rows(value, m, k)[:, j * lanes:(j + 1) * lanes]

    def out_far(j):
        got(f"vu{j}", f"vd{j}")
        value = out_term(across, pl.ds(j * lanes, lanes))
        for k in range(2):
            for m in range(n_y):
                part[j, k, m] = part[j, k, m] + out_rows(value, m, k)
        copy(f"pair{j}", part.at[j, 1 - c], part_in.at[j], core)

    for j in range(2):
        events[f"wfar{j}"] = functools.partial(out_far, j)

    def scatter(key, dest, slots, m, n, up, dn, ready, done):
        last = n // 2 - 1

        def begin():
            ready()
            mid = lax.rem(m + n // 2, n)
            copy(key + "u0", dest(mid, 1), slots(0, 0, 1), up)
            copy(key + "d0", dest(mid, 2), slots(1, 0, 2), dn)

        def step(way, s):
            gap = n // 2 - s
            to = lax.rem(m + (n - gap if way else gap), n)
            k = 1 + way if s == 1 else 0
            name = "ud"[way]
            got(f"{key}{name}{s - 1}")
            dest(to, k)[...] = dest(to, k)[...] + slots(way, s - 1, k)[...]
            copy(f"{key}{name}{s}", dest(to, 0), slots(way, s, 0), dn if way else up)

        def finish():
            got(f"{key}u{last}", f"{key}d{last}")
            done(dest(m, 0)[...] + slots(0, last, 0)[...] + slots(1, last, 0)[...])

        events[key + "0"] = begin
        for s in range(1, last + 1):
            for way in range(2):
                events[f"{key}{'ud'[way]}{s}"] = functools.partial(step, way, s)
        events[f"{key}{last + 1}"] = finish

    row_parts = (pl.ds(0, rows), pl.ds(0, h), pl.ds(h, h))

    def out_ready(j):
        got(f"pair{j}")
        part[j, c] = part[j, c] + part_in[j]

    def out_done(j, value):
        out[:, j * lanes:(j + 1) * lanes] = value

    def out_scatter(j):
        scatter(f"yr{j}", lambda m, k: part.at[j, c, m, row_parts[k]], lambda way, s, k: (y_up, y_dn)[way].at[j, s, row_parts[k]],
                y, n_y, yu, yd, functools.partial(out_ready, j), functools.partial(out_done, j))

    out_scatter(0)
    out_scatter(1)

    pair, odd = t // 2, lax.rem(t, 2)
    unit = depth // 6
    own_at, other_at = pair * 3 * unit, (1 - pair) * 3 * unit
    first_at, last_at = other_at + 2 * unit * (1 - odd), other_at + unit * odd
    zlo_parts = (pl.ds(0, 2), pl.ds(0, 1), pl.ds(1, 1))

    def ga_store(buffer, blocks):
        value = dot3(halves(grads[0]), halves(blocks), 1, 1)
        for m in range(n_x):
            for z in range(2):
                buffer[m, z] = value[(z * n_x + m) * rows:(z * n_x + m + 1) * rows]

    def ga_early():
        ga_store(early[0], jnp.concatenate([tile[aligned(own_at, 3 * unit)], tile[aligned(first_at, unit)]], 0))

    def ga_late():
        ga_store(late[0], tile[aligned(last_at, 2 * unit)])

    def ga_scatter(key, swapped, buffers, ready):
        buffer, up_in, dn_in, swap, swap_in = buffers

        def done(value):
            swap[...] = value
            copy(swapped, swap.at[1 - zl], swap_in, zlo)

        scatter(key, lambda m, j: buffer.at[m, zlo_parts[j]], lambda way, s, j: (up_in, dn_in)[way].at[s, zlo_parts[j]],
                x, n_x, xu, xd, ready, done)

    ga_scatter("x0", "l0", early, ga_early)
    events["g1"] = ga_late
    ga_scatter("x10", "l1", late, lambda: None)

    @event("gwa")
    def _():
        own = pl.ds(pl.multiple_of(t * w_rows, 16), w_rows)
        grad_weight[...] = dot3((acts_hi[own], acts_lo[own]), halves(grads[0]), 1, 0)

    def gw_add(*slots):
        total = grad_weight[...]
        for slot in slots:
            total = total + dot3(halves(cols[slot]), halves(grads[slot]), 1, 0)
        grad_weight[...] = total

    events["gwb"] = functools.partial(gw_add, 1, 2)
    events["gwc"] = functools.partial(gw_add, 3)

    def columns(start, count):
        return pl.ds(pl.multiple_of(start, unit), count)

    @event("end")
    def _():
        got("l0")
        value = early[3][zl] + early[4][...]
        grad_acts[:, columns(own_at, 3 * unit)] = value[:, :3 * unit]
        grad_acts[:, columns(first_at, unit)] = value[:, 3 * unit:]
        got("l1")
        grad_acts[:, columns(last_at, 2 * unit)] = late[3][zl] + late[4][...]

    for name in ORDER:
        events.pop(name)()
    assert not events
    for sent in started:
        sent.wait_send()


def shards(sizes, acts, weight, grad_out):
    n_tok, n_fin, n_fout = sizes
    n_y, n_x = n_fin // 2, n_fout // 2
    toks, depth = acts.shape
    w_rows, width = weight.shape
    rows = grad_out.shape[0]
    unit = depth // 6

    def scattered(count):
        shapes = [(n_x, 2), (n_x // 2, 2), (n_x // 2, 2), (2,), ()]
        return [pltpu.VMEM((*shape, rows, count), F32) for shape in shapes]

    vmem = pl.BlockSpec(memory_space=pltpu.VMEM)
    return pl.pallas_call(
        functools.partial(kernel, sizes),
        out_shape=(
            jax.ShapeDtypeStruct((rows, width), F32),
            jax.ShapeDtypeStruct((rows, depth), F32),
            jax.ShapeDtypeStruct((w_rows, width), F32),
        ),
        in_specs=[pl.BlockSpec(memory_space=pl.ANY)] * 3,
        out_specs=(vmem,) * 3,
        scratch_shapes=[
            pltpu.VMEM((toks, depth), F32),
            pltpu.VMEM((depth, toks), F32),
            pltpu.VMEM((depth, toks), jnp.bfloat16),
            pltpu.VMEM((depth, toks), jnp.bfloat16),
            pltpu.VMEM((n_tok, w_rows, toks), F32),
            pltpu.VMEM((n_tok, toks, width), F32),
            pltpu.VMEM((n_tok * w_rows, width), F32),
            pltpu.VMEM((2, 2, n_y, rows, width // 2), F32),
            pltpu.VMEM((2, n_y, rows, width // 2), F32),
            pltpu.VMEM((2, n_y // 2, rows, width // 2), F32),
            pltpu.VMEM((2, n_y // 2, rows, width // 2), F32),
            scattered(4 * unit),
            scattered(2 * unit),
            pltpu.SemaphoreType.DMA((128,)),
            pltpu.SemaphoreType.DMA((128,)),
            pltpu.SemaphoreType.DMA((3,)),
        ],
        compiler_params=pltpu.CompilerParams(collective_id=0, has_side_effects=True, vmem_limit_bytes=54 * 2**20),
    )(acts, weight, grad_out)


def solution(mesh):
    sizes = tuple(mesh.shape[name] for name in ("tok", "fin", "fout"))
    in_specs = (P("tok", "fin"), P(("fin", "tok"), "fout"), P(("tok", "fin"), "fout"))
    out_specs = (P(("tok", "fin"), "fout"), P(("tok", "fout"), "fin"), P(("fin", "tok"), "fout"))
    return jax.shard_map(functools.partial(shards, sizes), mesh=mesh, in_specs=in_specs, out_specs=out_specs, check_vma=False)
```

```python
import functools

import jax
import jax.numpy as jnp
from jax import lax
from jax.experimental import pallas as pl
from jax.experimental.pallas import tpu as pltpu
from jax.sharding import PartitionSpec as P

MESH = pl.DeviceIdType.MESH
F32 = jnp.float32

ORDER = (
    "zg0", "ya0", "w01", "a0", "zfu", "w00", "zfd", "yad1", "yau1", "yb0", "w03", "xa0", "w02", "xau1", "xad1",
    "yau2", "yad2", "ybu1", "xau2", "yad3", "xad2", "yau3", "wfu0", "yc0", "wfd0", "xad3", "as", "ya4", "ycd1",
    "wfd1", "ycu1", "ybu2", "wfu1", "ybd1", "wn", "xau3", "yaw", "x00", "ycu2", "ybd2", "ycd2", "x0u1", "xa4",
    "ybu3", "ycu3", "x0d1", "wfar0", "wfar1", "g1", "x100", "x0u2", "yr00", "yr10", "ybd3", "x10d1", "x10u1",
    "x0d2", "yr0u1", "ycd3", "yr1d1", "yr1u1", "yr0d1", "x10u2", "x10d2", "yr0u2", "x0u3", "x0d3", "yr1u2", "yr0d2",
    "yr1d2", "x10u3", "x10d3", "yb4", "yc4", "yr0u3", "yr1u3", "yr0d3", "x04", "ybw", "yr1d3", "ycw", "x104", "gw",
    "yr14", "yr04", "end",
)


def halves(value):
    high = value.astype(jnp.bfloat16)
    return high, (value - high.astype(F32)).astype(jnp.bfloat16)


def dot3(left, right, left_dim, right_dim):
    dims = (((left_dim,), (right_dim,)), ((), ()))
    dot = functools.partial(lax.dot_general, dimension_numbers=dims, preferred_element_type=F32)
    return dot(left[0], right[0]) + (dot(left[0], right[1]) + dot(left[1], right[0]))


def kernel(sizes, acts_in, weight_in, grad_in, out, grad_acts, grad_weight,
           acts, acts_t, acts_hi, acts_lo, cols, grads, tile, part, part_in, y_up, y_dn, early, late, send_sem, recv_sem, local_sem):
    n_tok, n_fin, n_fout = sizes
    n_y, n_x = n_fin // 2, n_fout // 2
    t, i, o = lax.axis_index("tok"), lax.axis_index("fin"), lax.axis_index("fout")
    y, c = i // 2, lax.rem(i, 2)
    zl, x = o // n_x, lax.rem(o, n_x)
    z_up, z_dn = [(lax.rem(t + d, n_tok), i, o) for d in (1, n_tok - 1)]
    yu, yd = [(t, lax.rem(i + d, n_fin), o) for d in (2, n_fin - 2)]
    core = (t, i + 1 - 2 * c, o)
    xu, xd = [(t, i, zl * n_x + lax.rem(x + d, n_x)) for d in (1, n_x - 1)]
    zlo = (t, i, lax.rem(o + n_x, n_fout))
    z_op = (lax.rem(t + 2, n_tok), i, lax.rem(o + n_x, n_fout))
    rows, w_rows = grad_in.shape[0], weight_in.shape[0]
    piece = w_rows // n_x
    depth, width = acts_in.shape[1], weight_in.shape[1]
    lanes = width // 2
    w_half = w_rows // 2

    def aligned(start, count):
        return pl.ds(pl.multiple_of(start, 8), count)

    mine = aligned(i * rows, rows)
    loads = [
        pltpu.make_async_copy(grad_in, grads.at[0, mine], local_sem.at[0]),
        pltpu.make_async_copy(weight_in, tile.at[aligned(t * w_rows, w_rows)], local_sem.at[1]),
        pltpu.make_async_copy(acts_in, acts, local_sem.at[2]),
    ]
    for load in loads:
        load.start()

    barrier = pltpu.get_barrier_semaphore()
    peers = (z_up, z_dn, z_op, yu, yd, core, xu, xd, zlo)
    for peer in peers:
        pl.semaphore_signal(barrier, inc=1, device_id=peer, device_id_type=MESH)
    pl.semaphore_wait(barrier, len(peers))
    for load in loads:
        load.wait()

    started = []
    cp = {}
    events = {}

    def copy(key, src, dst, peer):
        k = len(started)
        cp[key] = pltpu.make_async_remote_copy(src_ref=src, dst_ref=dst, send_sem=send_sem.at[k], recv_sem=recv_sem.at[k],
                                               device_id=peer, device_id_type=MESH)
        cp[key].start()
        started.append(cp[key])

    waited = set()

    def got(*keys):
        for key in keys:
            if key not in waited:
                waited.add(key)
                cp[key].wait_recv()

    def event(name):
        def add(run):
            events[name] = run
            return run
        return add


    h = rows // 2
    first, second = aligned(i * rows, h), aligned(i * rows + h, h)

    @event("zg0")
    def _():
        copy("zgu", grads.at[0, mine], grads.at[2, mine], z_up)
        copy("zgd", grads.at[0, mine], grads.at[1, mine], z_dn)

    @event("zfu")
    def _():
        got("zgu")
        copy("zgu2", grads.at[2, first], grads.at[3, first], z_up)

    @event("zfd")
    def _():
        got("zgd")
        copy("zgd2", grads.at[1, second], grads.at[3, second], z_dn)

    def gather(key, piece_of, m, n, up, dn, to_core, need):
        last = n // 2

        def begin():
            got(*need)
            copy(key + "u1", piece_of(m, 0), piece_of(m, 0), up)
            copy(key + "d1", piece_of(m, 0), piece_of(m, 0), dn)
            if to_core:
                copy(key + "c", piece_of(m, 0), piece_of(m, 0), core)

        def step(way, s):
            back = lax.rem(m + (n - s if way == "u" else s), n)
            got(f"{key}{way}{s}")
            k = 0 if s + 1 < last else (1 if way == "u" else 2)
            copy(f"{key}{way}{s + 1}", piece_of(back, k), piece_of(back, k), up if way == "u" else dn)
            if to_core:
                copy(f"{key}c{way}{s}", piece_of(back, 0), piece_of(back, 0), core)

        def finish():
            got(f"{key}u{last}", f"{key}d{last}")
            if to_core:
                back = lax.rem(m + last, n)
                copy(f"{key}c{last}", piece_of(back, 0), piece_of(back, 0), core)

        events[key + "0"] = begin
        for s in range(1, last):
            for way in "ud":
                events[f"{key}{way}{s}"] = functools.partial(step, way, s)
        events[f"{key}{last}"] = finish
        if to_core:
            inner = [f"{key}c{way}{s}" for s in range(1, last) for way in "ud"]
            events[key + "w"] = lambda: got(key + "c", *inner, f"{key}c{last}")

    def grad_rows(slots):
        def piece_of(m, k):
            base = (2 * m + c) * rows
            return grads.at[slots, (aligned(base, rows), aligned(base, h), aligned(base + h, h))[k]]
        return piece_of

    gather("ya", grad_rows(pl.ds(0, 1)), y, n_y, yu, yd, True, ())
    gather("yb", grad_rows(pl.ds(1, 2)), y, n_y, yu, yd, True, ())
    gather("yc", grad_rows(pl.ds(3, 1)), y, n_y, yu, yd, True, ("zgu2", "zgd2"))

    def cols_of(m, k):
        cut = 16
        base = m * piece
        return cols.at[pl.ds(1, n_tok - 1), (aligned(base, piece), aligned(base, cut), aligned(base + cut, piece - cut))[k]]

    gather("xa", cols_of, x, n_x, xu, xd, False, ("a1", "a3", "a2"))

    @event("a0")
    def _():
        acts_t[...] = acts[...].T
        for d, slot, peer in ((1, 2, z_up), (3, 1, z_dn), (2, 3, z_op)):
            span = aligned(lax.rem(t + d, n_tok) * w_rows + x * piece, piece)
            copy(f"a{d}", acts_t.at[span], cols.at[slot, aligned(x * piece, piece)], peer)

    @event("as")
    def _():
        acts_hi[...], acts_lo[...] = halves(acts_t[...])

    before, after, across = [lax.rem(t + d, n_tok) for d in (n_tok - 1, 1, 2)]

    def w_part(block, k):
        return tile.at[aligned(block * w_rows + k // 2 * w_half, w_half), pl.ds(k % 2 * lanes, lanes)]

    def w_first(k):
        other = (k + 2) % 4
        copy(f"wu{k}", w_part(t, k), w_part(t, k), z_up)
        copy(f"wd{k}", w_part(t, other), w_part(t, other), z_dn)

    def w_up(k):
        got(f"wu{k}")
        copy(f"vu{k}", w_part(before, k), w_part(before, k), z_up)

    def w_dn(k):
        got(f"wd{k}")
        copy(f"vd{k}", w_part(after, k + 2), w_part(after, k + 2), z_dn)

    for k in range(4):
        events[f"w0{k}"] = functools.partial(w_first, k)
    for k in range(2):
        events[f"wfu{k}"] = functools.partial(w_up, k)
        events[f"wfd{k}"] = functools.partial(w_dn, k)

    def out_term(block, columns):
        span = pl.ds(pl.multiple_of(block * w_rows, 16), w_rows)
        return dot3((acts_hi[span], acts_lo[span]), halves(tile[aligned(block * w_rows, w_rows), columns]), 0, 0)

    def out_rows(value, m, k):
        return value[(2 * m + k) * rows:(2 * m + k + 1) * rows]

    @event("wn")
    def _():
        got(*[f"w{way}{k}" for way in "ud" for k in range(4)])
        value = out_term(t, pl.ds(0, width)) + out_term(before, pl.ds(0, width)) + out_term(after, pl.ds(0, width))
        for j in range(2):
            for m in range(n_y):
                for k in range(2):
                    part[j, k, m] = out_rows(value, m, k)[:, j * lanes:(j + 1) * lanes]

    def out_far(j):
        got(f"vu{j}", f"vd{j}")
        value = out_term(across, pl.ds(j * lanes, lanes))
        for k in range(2):
            for m in range(n_y):
                part[j, k, m] = part[j, k, m] + out_rows(value, m, k)
        copy(f"pair{j}", part.at[j, 1 - c], part_in.at[j], core)

    for j in range(2):
        events[f"wfar{j}"] = functools.partial(out_far, j)

    def scatter(key, dest, slots, m, n, up, dn, ready, done):
        last = n // 2 - 1

        def begin():
            ready()
            mid = lax.rem(m + n // 2, n)
            copy(key + "u0", dest(mid, 1), slots(0, 0, 1), up)
            copy(key + "d0", dest(mid, 2), slots(1, 0, 2), dn)

        def step(way, s):
            gap = n // 2 - s
            to = lax.rem(m + (n - gap if way else gap), n)
            k = 1 + way if s == 1 else 0
            name = "ud"[way]
            got(f"{key}{name}{s - 1}")
            dest(to, k)[...] = dest(to, k)[...] + slots(way, s - 1, k)[...]
            copy(f"{key}{name}{s}", dest(to, 0), slots(way, s, 0), dn if way else up)

        def finish():
            got(f"{key}u{last}", f"{key}d{last}")
            done(dest(m, 0)[...] + slots(0, last, 0)[...] + slots(1, last, 0)[...])

        events[key + "0"] = begin
        for s in range(1, last + 1):
            for way in range(2):
                events[f"{key}{'ud'[way]}{s}"] = functools.partial(step, way, s)
        events[f"{key}{last + 1}"] = finish

    row_parts = (pl.ds(0, rows), pl.ds(0, h), pl.ds(h, h))

    def out_ready(j):
        got(f"pair{j}")
        part[j, c] = part[j, c] + part_in[j]

    def out_done(j, value):
        out[:, j * lanes:(j + 1) * lanes] = value

    def out_scatter(j):
        scatter(f"yr{j}", lambda m, k: part.at[j, c, m, row_parts[k]], lambda way, s, k: (y_up, y_dn)[way].at[j, s, row_parts[k]],
                y, n_y, yu, yd, functools.partial(out_ready, j), functools.partial(out_done, j))

    out_scatter(0)
    out_scatter(1)

    pair, odd = t // 2, lax.rem(t, 2)
    unit = depth // 6
    own_at, other_at = pair * 3 * unit, (1 - pair) * 3 * unit
    first_at, last_at = other_at + 2 * unit * (1 - odd), other_at + unit * odd
    zlo_parts = (pl.ds(0, 2), pl.ds(0, 1), pl.ds(1, 1))

    def ga_store(buffer, blocks):
        value = dot3(halves(grads[0]), halves(blocks), 1, 1)
        for m in range(n_x):
            for z in range(2):
                buffer[m, z] = value[(z * n_x + m) * rows:(z * n_x + m + 1) * rows]

    def ga_early():
        ga_store(early[0], jnp.concatenate([tile[aligned(own_at, 3 * unit)], tile[aligned(first_at, unit)]], 0))

    def ga_late():
        ga_store(late[0], tile[aligned(last_at, 2 * unit)])

    def ga_scatter(key, swapped, buffers, ready):
        buffer, up_in, dn_in, swap, swap_in = buffers

        def done(value):
            swap[...] = value
            copy(swapped, swap.at[1 - zl], swap_in, zlo)

        scatter(key, lambda m, j: buffer.at[m, zlo_parts[j]], lambda way, s, j: (up_in, dn_in)[way].at[s, zlo_parts[j]],
                x, n_x, xu, xd, ready, done)

    ga_scatter("x0", "l0", early, ga_early)
    events["g1"] = ga_late
    ga_scatter("x10", "l1", late, lambda: None)

    @event("gw")
    def _():
        own = pl.ds(pl.multiple_of(t * w_rows, 16), w_rows)
        total = dot3((acts_hi[own], acts_lo[own]), halves(grads[0]), 1, 0)
        for slot in range(1, n_tok):
            total = total + dot3(halves(cols[slot]), halves(grads[slot]), 1, 0)
        grad_weight[...] = total

    def columns(start, count):
        return pl.ds(pl.multiple_of(start, unit), count)

    @event("end")
    def _():
        got("l0")
        value = early[3][zl] + early[4][...]
        grad_acts[:, columns(own_at, 3 * unit)] = value[:, :3 * unit]
        grad_acts[:, columns(first_at, unit)] = value[:, 3 * unit:]
        got("l1")
        grad_acts[:, columns(last_at, 2 * unit)] = late[3][zl] + late[4][...]

    for name in ORDER:
        events.pop(name)()
    assert not events
    for sent in started:
        sent.wait_send()


def shards(sizes, acts, weight, grad_out):
    n_tok, n_fin, n_fout = sizes
    n_y, n_x = n_fin // 2, n_fout // 2
    toks, depth = acts.shape
    w_rows, width = weight.shape
    rows = grad_out.shape[0]
    unit = depth // 6

    def scattered(count):
        shapes = [(n_x, 2), (n_x // 2, 2), (n_x // 2, 2), (2,), ()]
        return [pltpu.VMEM((*shape, rows, count), F32) for shape in shapes]

    vmem = pl.BlockSpec(memory_space=pltpu.VMEM)
    return pl.pallas_call(
        functools.partial(kernel, sizes),
        out_shape=(
            jax.ShapeDtypeStruct((rows, width), F32),
            jax.ShapeDtypeStruct((rows, depth), F32),
            jax.ShapeDtypeStruct((w_rows, width), F32),
        ),
        in_specs=[pl.BlockSpec(memory_space=pl.ANY)] * 3,
        out_specs=(vmem,) * 3,
        scratch_shapes=[
            pltpu.VMEM((toks, depth), F32),
            pltpu.VMEM((depth, toks), F32),
            pltpu.VMEM((depth, toks), jnp.bfloat16),
            pltpu.VMEM((depth, toks), jnp.bfloat16),
            pltpu.VMEM((n_tok, w_rows, toks), F32),
            pltpu.VMEM((n_tok, toks, width), F32),
            pltpu.VMEM((n_tok * w_rows, width), F32),
            pltpu.VMEM((2, 2, n_y, rows, width // 2), F32),
            pltpu.VMEM((2, n_y, rows, width // 2), F32),
            pltpu.VMEM((2, n_y // 2, rows, width // 2), F32),
            pltpu.VMEM((2, n_y // 2, rows, width // 2), F32),
            scattered(4 * unit),
            scattered(2 * unit),
            pltpu.SemaphoreType.DMA((128,)),
            pltpu.SemaphoreType.DMA((128,)),
            pltpu.SemaphoreType.DMA((3,)),
        ],
        compiler_params=pltpu.CompilerParams(collective_id=0, has_side_effects=True, vmem_limit_bytes=54 * 2**20),
    )(acts, weight, grad_out)


def solution(mesh):
    sizes = tuple(mesh.shape[name] for name in ("tok", "fin", "fout"))
    in_specs = (P("tok", "fin"), P(("fin", "tok"), "fout"), P(("tok", "fin"), "fout"))
    out_specs = (P(("tok", "fin"), "fout"), P(("tok", "fout"), "fin"), P(("fin", "tok"), "fout"))
    return jax.shard_map(functools.partial(shards, sizes), mesh=mesh, in_specs=in_specs, out_specs=out_specs, check_vma=False)
```
